32 devices in a mesh: group: 2 (over y), ctx: 16 (over z, x, core).
Axes of the slice: x: 2, y: 2, z: 4, core: 2. Of those that a mesh axis runs over, the one named last changes fastest.
Arguments:
- queries: bfloat16 [2048, 64, 320], P(('group', 'ctx')), parts along dimension 0, may hold values from -32 to 32
- latent_keys: bfloat16 [2048, 320], P(('group', 'ctx')), parts along dimension 0, may hold values from -4 to 4
- hidden: bfloat16 [2048, 3584], P(('group', 'ctx')), parts along dimension 0, may hold values from -6 to 6
- routes: int32 [2048, 2], P(('group', 'ctx')), parts along dimension 0, may hold values from 0 to 3, all different within a row; in each aligned block of 64 rows (0 to 63, 64 to 127, ...) at most 40 rows name the same one
- route_weights: float32 [2048, 2], P(('group', 'ctx')), parts along dimension 0, may hold values from 0.05 to 0.5
- w_gate: bfloat16 [16, 3584, 256], P('ctx'), may hold values from -0.09375 to 0.09375
- w_up: bfloat16 [16, 3584, 256], P('ctx'), may hold values from -0.09375 to 0.09375
- w_down: bfloat16 [16, 256, 3584], P('ctx'), may hold values from -0.1875 to 0.1875
Outputs:
- attended: bfloat16 [2048, 64, 256], P(('group', 'ctx')), parts along dimension 0
- mixed: bfloat16 [2048, 3584], P(('group', 'ctx')), parts along dimension 0
The draws below stay inside these ranges and needn't reach their ends.
There are 2 independent parts, one for each index of `group`. The reference program is written for one: setup_inputs(seed, part) draws one part's arguments, and reference() takes and returns one part's arrays. A program takes and returns all parts, laid end to end along the dimension named above; an argument that names none is the same for every part. Nothing has to cross between parts.
Inputs may be any that keep to these rules, and one draw needn't show every extreme that they name: `routes`: each row names 2 different experts; among the rows of one device no expert is named more than 40 times, a bound that some block reaches.
All inputs are finite; a program needn't handle non-finite values.
Results may differ from the reference program's by a relative error of at most 0.0059.
Values may be sent and summed in bfloat16 or wider, within the bound.
A program may use at most 128 MiB of HBM per device.

```python
import math
import jax
import jax.numpy as jnp
import numpy as np
from jax import lax

H = 64
LAT = 256
ROPE = 64
NOPE_DIM = 128
D = 3584
FF = 1024
SPLIT = 4
TOPK = 2
TOK_DEV = 64
EXPERTS = 4
TOKENS = 1024
SEQ_LEN = 1024
SEQS = 1
MOST = 40
FF_DEV = 256
N_CTX = 16


def draw_latent_keys(key, part):
    key = jax.random.fold_in(key, 11)
    values = jnp.clip(jax.random.normal(key, (TOKENS, LAT + ROPE), jnp.float32), -4.0, 4.0)
    return values.astype(jnp.bfloat16)


def draw_queries(key, part):
    key = jax.random.fold_in(key, 12)
    shape = (TOKENS, H, LAT + ROPE)
    values = 1.2 * jnp.clip(jax.random.normal(key, shape, jnp.float32), -4.0, 4.0)
    return values.astype(jnp.bfloat16)


def block_scale(stream_key, shape, split, least, high):
    loudness, own = 1.0, jax.random.fold_in(stream_key, 6)
    for dim, shards_of in split:
        heights = jnp.exp(jax.random.uniform(jax.random.fold_in(own, dim), (shards_of,), jnp.float32, least / len(split), high / len(split)))
        loudness = loudness * jnp.repeat(heights, shape[dim] // shards_of).reshape([-1 if axis == dim else 1 for axis in range(len(shape))])
    return loudness


def routed_block(own_key, own, number, rows, amount, top, bound, slope):
    sequence = jax.random.permutation(own_key, amount)
    heavy_load, usual = shares(amount, rows * top, bound, slope, True), shares(amount, rows * top, bound, slope, False)
    places = jnp.arange(amount)

    def named(sizes, rotation):
        used = int((sizes > 0).sum())
        fixed = max(1, used // 4)
        passed = fixed + (places - fixed + rotation * (used - fixed)) % max(1, amount - fixed)
        return jnp.zeros((amount,), jnp.int32).at[sequence[jnp.where(places < fixed, places, passed)]].set(jnp.asarray(sizes, jnp.int32))

    sizes = jnp.where(number % 4 == 0, named(heavy_load, number // 4), named(usual, number - number // 4 - 1))
    mixed = jax.random.permutation(jax.random.fold_in(own, 3), amount)
    source_of, taker = mixed[0:amount // 2 * 2:2], mixed[1:amount // 2 * 2:2]
    margin = jnp.minimum(sizes[source_of] - 1, bound - sizes[taker]) // 2
    margin = jnp.where((source_of == sequence[0]) | (taker == sequence[0]) | (sizes[taker] == 0), 0, jnp.maximum(margin, 0))
    passed = jax.random.randint(jax.random.fold_in(own, 4), (amount // 2,), 0, 1 << 20) % (margin + 1)
    sizes = sizes.at[source_of].add(-passed).at[taker].add(passed)
    members = jnp.searchsorted(jnp.cumsum(sizes), jnp.arange(rows * top), side="right").astype(jnp.int32)
    listing = members.reshape(top, rows).T
    listing = listing[jax.random.permutation(jax.random.fold_in(own, 1), rows)]
    rotation = jax.random.randint(jax.random.fold_in(own, 2), (rows, 1), 0, top)
    return jnp.take_along_axis(listing, (jnp.arange(top)[None, :] + rotation) % top, axis=1)


def shares(amount, total, most, slope, full):
    portions = [(1 << 20) // math.isqrt(standing ** slope) + 1 for standing in range(1, amount + 1)]
    largest = most if full else min(most, max(-(-total // amount), total * portions[0] // sum(portions)))
    least = 1 if total - largest >= amount - 1 else 0
    given, surplus = [largest] + [least] * (amount - 1), total - largest - least * (amount - 1)
    while surplus > 0:
        movable = [i for i in range(1, amount) if given[i] < largest] or [i for i in range(1, amount) if given[i] < most]
        pool, left = sum([portions[i] for i in movable]), surplus
        for i in movable:
            addition = min(most - given[i], max(1, left * portions[i] // pool), surplus)
            given[i] = given[i] + addition
            surplus = surplus - addition
    return np.array(given)


def bell_draw(key, shape, spread, reach, cuts=(), kind=jnp.bfloat16):
    values = spread * jax.random.normal(key, shape, jnp.float32)
    if cuts:
        values = values * block_scale(key, shape, cuts, -0.22, 0.18)
    return jnp.clip(values, -reach, reach).astype(kind)


def setup_inputs(seed: int = 0, part: int = 0) -> dict:
    streams_of = jax.random.split(jax.random.key(seed), 9)
    part_keys = jax.random.split(jax.random.fold_in(streams_of[8], part), 9)
    queries = draw_queries(jax.random.fold_in(jax.random.fold_in(streams_of[8], part), 71), part)
    latent_keys = draw_latent_keys(jax.random.fold_in(jax.random.fold_in(streams_of[8], part), 71), part)
    hidden = bell_draw(part_keys[2], (TOKENS, D), 1.0, 6.0, ((0, 16),))
    routes_keys = jax.random.split(jax.random.fold_in(part_keys[3], 1), TOKENS // TOK_DEV)
    routes_turns = jax.random.permutation(jax.random.fold_in(part_keys[3], 3), TOKENS // TOK_DEV)
    routes = jax.vmap(lambda own, number: routed_block(jax.random.fold_in(part_keys[3], 2), own, number, TOK_DEV, EXPERTS, TOPK, MOST, 1))(routes_keys, routes_turns).reshape((TOKENS, TOPK))
    route_weights = jnp.clip(jnp.exp(math.log(0.5) - 2.3025851 * jax.random.uniform(part_keys[4], (TOKENS, TOPK), jnp.float32) ** block_scale(part_keys[4], (TOKENS, TOPK), ((0, 16),), -0.2, 0.2)), 0.05, 0.5)
    w_gate = bell_draw(streams_of[5], (EXPERTS * SPLIT, D, FF_DEV), D ** -0.5, 0.09375, ((0, 16),))
    w_up = bell_draw(streams_of[6], (EXPERTS * SPLIT, D, FF_DEV), D ** -0.5, 0.09375, ((0, 16),))
    w_down = bell_draw(streams_of[7], (EXPERTS * SPLIT, FF_DEV, D), FF ** -0.5, 0.1875, ((0, 16),))
    return dict(queries=queries, latent_keys=latent_keys, hidden=hidden, routes=routes, route_weights=route_weights, w_gate=w_gate, w_up=w_up, w_down=w_down)


def sequence_attention(queries, latent_keys):
    score_scale = 1.0 / math.sqrt(NOPE_DIM + ROPE)
    key_table = latent_keys.astype(jnp.float32)
    value_table = key_table[:, :LAT]
    block_rows = 64
    key_pos = jnp.arange(SEQ_LEN, dtype=jnp.int32)

    def one_block(block_start):
        query_block = lax.dynamic_slice_in_dim(queries, block_start, block_rows, 0).astype(jnp.float32)
        scores = jnp.einsum('qhd,kd->qhk', query_block, key_table) * score_scale
        query_pos = block_start + jnp.arange(block_rows, dtype=jnp.int32)
        allowed = key_pos[None, :] <= query_pos[:, None]
        scores = jnp.where(allowed[:, None, :], scores, -jnp.inf)
        peak = lax.optimization_barrier(jnp.max(scores, axis=-1, keepdims=True))
        expo = jnp.exp(scores - peak)
        totals = lax.optimization_barrier(jnp.sum(expo, axis=-1))
        probs = lax.optimization_barrier(expo.astype(jnp.bfloat16)).astype(jnp.float32)
        summed = jnp.einsum('qhk,kd->qhd', probs, value_table)
        return (summed / totals[..., None]).astype(jnp.bfloat16)
    starts = jnp.arange(SEQ_LEN // block_rows, dtype=jnp.int32) * block_rows
    blocks = lax.map(one_block, starts)
    return blocks.reshape(SEQ_LEN, H, LAT)

def attention_part(queries, latent_keys):
    query_seqs = queries.reshape(SEQS, SEQ_LEN, H, LAT + ROPE)
    key_seqs = latent_keys.reshape(SEQS, SEQ_LEN, LAT + ROPE)
    outputs = lax.map(lambda pair: sequence_attention(pair[0], pair[1]), (query_seqs, key_seqs))
    return outputs.reshape(TOKENS, H, LAT)

def expert_part(hidden, routes, route_weights, w_gate, w_up, w_down):
    per_device = routes.reshape(N_CTX, TOK_DEV * TOPK)
    onehot = (per_device[..., None] == jnp.arange(EXPERTS, dtype=jnp.int32)).astype(jnp.int32)
    rank = lax.optimization_barrier(jnp.sum((jnp.cumsum(onehot, axis=1) - onehot) * onehot, axis=-1))
    slot = (jnp.arange(N_CTX, dtype=jnp.int32)[:, None] * MOST + rank).reshape(TOKENS, TOPK).astype(jnp.int32)
    capacity = N_CTX * MOST
    token_index = jnp.broadcast_to(jnp.arange(TOKENS, dtype=jnp.int32)[:, None], (TOKENS, TOPK))
    token_of = jnp.zeros((EXPERTS, capacity), jnp.int32).at[routes, slot].set(token_index)
    weight_of = jnp.zeros((EXPERTS, capacity), jnp.float32).at[routes, slot].set(route_weights)

    def expert_step(running, expert):
        picked = token_of[expert]
        token_block = hidden[picked]
        total = jnp.zeros((capacity, D), jnp.float32)
        for piece_index in range(SPLIT):
            row_index = (expert * SPLIT + piece_index).astype(jnp.int32)
            gate_rows = lax.dynamic_index_in_dim(w_gate, row_index, 0, keepdims=False)
            up_rows = lax.dynamic_index_in_dim(w_up, row_index, 0, keepdims=False)
            down_rows = lax.dynamic_index_in_dim(w_down, row_index, 0, keepdims=False)
            gate = jnp.dot(token_block, gate_rows, preferred_element_type=jnp.float32)
            upper = jnp.dot(token_block, up_rows, preferred_element_type=jnp.float32)
            units = (jax.nn.silu(gate) * upper).astype(jnp.bfloat16)
            partial_value = jnp.dot(units, down_rows, preferred_element_type=jnp.float32).astype(jnp.bfloat16)
            total = total + lax.optimization_barrier(partial_value).astype(jnp.float32)
        running = running.at[picked].add(weight_of[expert][:, None] * total)
        return (running, None)
    start_value = jnp.zeros((TOKENS, D), jnp.float32)
    summed, unused = lax.scan(expert_step, start_value, jnp.arange(EXPERTS, dtype=jnp.int32))
    return summed.astype(jnp.bfloat16)

def reference(queries, latent_keys, hidden, routes, route_weights, w_gate, w_up, w_down):
    attended = attention_part(queries, latent_keys)
    mixed = expert_part(hidden, routes, route_weights, w_gate, w_up, w_down)
    return (attended, mixed)
```

```python
import functools
import math

import jax
import jax.numpy as jnp
from jax import lax
from jax.experimental import pallas as pl
from jax.experimental.pallas import tpu as pltpu
from jax.sharding import PartitionSpec as P

LAT = 256
ROPE = 64
NOPE_DIM = 128
SPLIT = 4
TOPK = 2
ROWS = 512


def layer_kernel(
    experts, q_hbm, keys_ref, hid_ref, sel_ref, comb_ref, wg_hbm, wu_hbm, wd_hbm,
    att_ref, mix_ref,
    q_v, wg, wu, wd, recv, own, part, cbuf, xbuf, ret, kbuf, acc, m_ref, l_ref,
    local_sem, sz, rz, skz, rkz, sx, rx, skx, rkx, sc, rc, skc, rkc,
    src_, rrc, srx, rrx, srz, rrz,
):
    E = experts
    slots = sel_ref.shape[1]
    toks = keys_ref.shape[0]
    D = hid_ref.shape[1]
    row_total = q_v.shape[0]
    heads = row_total // toks
    width = 512
    me = lax.axis_index("ctx")
    e = me // SPLIT
    s = me % SPLIT
    p = s // 2
    c = s % 2
    s_x = (1 - p) * 2 + c
    dev_x = e * SPLIT + s_x
    dev_c = e * SPLIT + p * 2 + (1 - c)

    def remote(src, dst, ssem, rsem, dev):
        return pltpu.make_async_remote_copy(
            src_ref=src, dst_ref=dst, send_sem=ssem, recv_sem=rsem,
            device_id={"ctx": dev}, device_id_type=pl.DeviceIdType.MESH,
        )

    barrier = pltpu.get_barrier_semaphore()

    def greet(k, _):
        pl.semaphore_signal(
            barrier, inc=1, device_id={"ctx": (e + k) % E * SPLIT + s},
            device_id_type=pl.DeviceIdType.MESH,
        )
        return 0

    lax.fori_loop(1, E, greet, 0)
    for dev in (dev_x, dev_c):
        pl.semaphore_signal(
            barrier, inc=1, device_id={"ctx": dev}, device_id_type=pl.DeviceIdType.MESH
        )
    loads = [
        pltpu.make_async_copy(q_hbm, q_v, local_sem.at[0]),
        pltpu.make_async_copy(wg_hbm, wg, local_sem.at[1]),
        pltpu.make_async_copy(wu_hbm, wu, local_sem.at[2]),
        pltpu.make_async_copy(wd_hbm, wd, local_sem.at[3]),
    ]
    for load in loads:
        load.start()
    kbuf[me] = keys_ref[...]
    pl.semaphore_wait(barrier, E + 1)

    def copy_z(t, i_src):
        return remote(own.at[t], recv.at[me], sz.at[t], rz.at[i_src], t * SPLIT + s)

    def copy_kz(t, i_src):
        return remote(kbuf.at[me], kbuf.at[me], skz.at[t], rkz.at[i_src], t * SPLIT + s)

    def copy_x(g):
        b = g * SPLIT + s
        return remote(recv.at[b], recv.at[b], sx.at[g], rx.at[g], dev_x)

    def copy_kx(g):
        b = g * SPLIT + s
        return remote(kbuf.at[b], kbuf.at[b], skx.at[g], rkx.at[g], dev_x)

    def copy_c(g, far):
        b = g * SPLIT + (s_x if far else s)
        return remote(recv.at[b], recv.at[b], sc.at[2 * g + far], rc.at[2 * g + far], dev_c)

    def copy_kc(g, far):
        b = g * SPLIT + (s_x if far else s)
        return remote(kbuf.at[b], kbuf.at[b], skc.at[2 * g + far], rkc.at[2 * g + far], dev_c)

    def copy_rc(g, q):
        return remote(
            part.at[g * SPLIT + 2 * q + (1 - c)], cbuf.at[2 * g + q],
            src_.at[2 * g + q], rrc.at[2 * g + q], dev_c,
        )

    def copy_rx(g):
        return remote(part.at[g * SPLIT + s_x], xbuf.at[g], srx.at[g], rrx.at[g], dev_x)

    def copy_rz(g, i_src):
        return remote(
            part.at[g * SPLIT + s], ret.at[e], srz.at[g], rrz.at[i_src], g * SPLIT + s
        )

    def dispatch(k, _):
        t = (e + k) % E
        copy_kz(t, e).start()
        own[t] = jnp.dot(
            sel_ref[t], hid_ref[...], preferred_element_type=jnp.float32
        ).astype(jnp.bfloat16)
        copy_z(t, e).start()
        return 0

    lax.fori_loop(1, E, dispatch, 0)
    recv[me] = jnp.dot(
        sel_ref[e], hid_ref[...], preferred_element_type=jnp.float32
    ).astype(jnp.bfloat16)

    def relay(k):
        g = (e + E - k) % E

        @pl.when(k > 0)
        def _():
            copy_kz(g, g).wait_recv()
            copy_z(g, g).wait_recv()

        copy_kx(g).start()
        copy_x(g).start()
        copy_kc(g, 0).start()
        copy_c(g, 0).start()
        copy_kx(g).wait_recv()
        copy_kc(g, 1).start()
        copy_x(g).wait_recv()
        copy_c(g, 1).start()

    def compute(k):
        g = (e + E - k) % E

        @pl.when(k == 0)
        def _():
            for load in loads[1:]:
                load.wait()

        copy_c(g, 0).wait_recv()
        copy_c(g, 1).wait_recv()
        rows = recv[pl.ds(g * SPLIT, SPLIT)].reshape(SPLIT * slots, D)
        gate = jnp.dot(rows, wg[...], preferred_element_type=jnp.float32)
        upper = jnp.dot(rows, wu[...], preferred_element_type=jnp.float32)
        units = (gate / (1.0 + jnp.exp(-gate)) * upper).astype(jnp.bfloat16)
        for start in range(0, D, width):
            piece = jnp.dot(
                units, wd[:, start : start + width], preferred_element_type=jnp.float32
            )
            part[pl.ds(g * SPLIT, SPLIT), :, start : start + width] = piece.astype(
                jnp.bfloat16
            ).reshape(SPLIT, slots, width)
        copy_rc(g, 0).start()
        copy_rc(g, 1).start()

    factor = math.log2(math.e) / math.sqrt(NOPE_DIM + ROPE)

    def attend(k):
        g = (e + E - k) % E
        copy_kc(g, 0).wait_recv()
        copy_kc(g, 1).wait_recv()

        def scores_of(r):
            keys = kbuf[pl.ds(g * SPLIT, SPLIT)].reshape(SPLIT * toks, LAT + ROPE)
            sc_ = lax.dot_general(
                q_v[pl.ds(r, ROWS)], keys, (((1,), (1,)), ((), ())),
                preferred_element_type=jnp.float32,
            )
            return sc_, keys[:, :LAT]

        @pl.when(k == 0)
        def _():
            loads[0].wait()

            def chunk(i, _):
                r = pl.multiple_of(i * ROWS, ROWS)
                sc_, vals = scores_of(r)
                tok = s * toks + (r + lax.broadcasted_iota(jnp.int32, sc_.shape, 0)) // heads
                col = lax.broadcasted_iota(jnp.int32, sc_.shape, 1)
                sc_ = jnp.where(col <= tok, sc_, -jnp.inf)
                m = jnp.max(sc_, axis=1, keepdims=True)
                ex = jnp.exp2((sc_ - m) * factor)
                m_ref[pl.ds(r, ROWS)] = m
                l_ref[pl.ds(r, ROWS)] = jnp.sum(ex, axis=1, keepdims=True)
                acc[pl.ds(r, ROWS)] = jnp.dot(
                    ex.astype(jnp.bfloat16), vals, preferred_element_type=jnp.float32
                )
                return 0

            lax.fori_loop(0, row_total // ROWS, chunk, 0)

        @pl.when(k > 0)
        def _():
            def chunk(i, _):
                r = pl.multiple_of(i * ROWS, ROWS)
                sc_, vals = scores_of(r)
                old = m_ref[pl.ds(r, ROWS)]
                m = jnp.maximum(old, jnp.max(sc_, axis=1, keepdims=True))
                ex = jnp.exp2((sc_ - m) * factor)
                fade = jnp.exp2((old - m) * factor)
                m_ref[pl.ds(r, ROWS)] = m
                l_ref[pl.ds(r, ROWS)] = l_ref[pl.ds(r, ROWS)] * fade + jnp.sum(
                    ex, axis=1, keepdims=True
                )
                acc[pl.ds(r, ROWS)] = acc[pl.ds(r, ROWS)] * fade + jnp.dot(
                    ex.astype(jnp.bfloat16), vals, preferred_element_type=jnp.float32
                )
                return 0

            lax.fori_loop(0, row_total // ROWS, chunk, 0)

        @pl.when(k == e)
        def _():
            def chunk(i, _):
                r = pl.multiple_of(i * ROWS, ROWS)
                att_ref[pl.ds(r, ROWS)] = (
                    acc[pl.ds(r, ROWS)] / l_ref[pl.ds(r, ROWS)]
                ).astype(jnp.bfloat16)
                return 0

            lax.fori_loop(0, row_total // ROWS, chunk, 0)

    def sum_cores(k):
        g = (e + E - k) % E
        copy_rc(g, 0).wait_recv()
        copy_rc(g, 1).wait_recv()
        b = g * SPLIT + s_x
        part[b] = (
            part[b].astype(jnp.float32) + cbuf[2 * g + (1 - p)].astype(jnp.float32)
        ).astype(jnp.bfloat16)
        copy_rx(g).start()

    def sum_chips(k):
        g = (e + E - k) % E
        copy_rx(g).wait_recv()
        b = g * SPLIT + s
        total = (
            part[b].astype(jnp.float32)
            + cbuf[2 * g + p].astype(jnp.float32)
            + xbuf[g].astype(jnp.float32)
        ).astype(jnp.bfloat16)

        @pl.when(k == 0)
        def _():
            ret[e] = total

        @pl.when(k > 0)
        def _():
            part[b] = total
            copy_rz(g, e).start()

    def step(i, _):
        @pl.when(i < E)
        def _():
            relay(i)

        @pl.when((i >= 1) & (i <= E))
        def _():
            compute(i - 1)

        @pl.when((i >= 2) & (i <= E + 1))
        def _():
            sum_cores(i - 2)

        @pl.when((i >= 1) & (i <= e + 1))
        def _():
            attend(i - 1)

        @pl.when(i >= 3)
        def _():
            sum_chips(i - 3)

        return 0

    lax.fori_loop(0, E + 3, step, 0)

    def unread(k, _):
        g = (e + E - k) % E
        copy_kc(g, 0).wait_recv()
        copy_kc(g, 1).wait_recv()
        return 0

    lax.fori_loop(e + 1, E, unread, 0)

    def arrive(k, _):
        g = (e + E - k) % E
        copy_rz(g, g).wait_recv()
        return 0

    lax.fori_loop(1, E, arrive, 0)
    for start in range(0, D, width):
        both = jnp.dot(
            comb_ref[...],
            ret[:, :, start : start + width].reshape(E * slots, width),
            preferred_element_type=jnp.float32,
        )
        mix_ref[:, start : start + width] = (both[:toks] + both[toks:]).astype(jnp.bfloat16)

    def sent(g, _):
        @pl.when(g != e)
        def _():
            copy_kz(g, e).wait_send()
            copy_z(g, e).wait_send()
            copy_rz(g, e).wait_send()

        copy_kx(g).wait_send()
        copy_x(g).wait_send()
        copy_rx(g).wait_send()
        for far in range(2):
            copy_kc(g, far).wait_send()
            copy_c(g, far).wait_send()
            copy_rc(g, far).wait_send()
        return 0

    lax.fori_loop(0, E, sent, 0)


def per_device(queries, latent_keys, hidden, routes, route_weights, w_gate, w_up, w_down):
    toks, heads, qw = queries.shape
    D = hidden.shape[1]
    ff = w_gate.shape[2]
    n_ctx = lax.axis_size("ctx")
    E = n_ctx // SPLIT
    most = toks * TOPK * 5 // (4 * E)
    slots = -(-most // 8) * 8
    flat = routes.reshape(-1)
    ids = jnp.arange(E, dtype=jnp.int32)
    onehot = (flat[:, None] == ids[None, :]).astype(jnp.int32)
    rank = jnp.sum((jnp.cumsum(onehot, axis=0) - onehot) * onehot, axis=1)
    slot = (flat * slots + rank).reshape(toks, TOPK)
    table = jnp.arange(E * slots, dtype=jnp.int32)
    hit = slot[:, :, None] == table[None, None, :]
    sel = (
        jnp.any(slot[None] == table[:, None, None], axis=2)
        .astype(jnp.bfloat16)
        .reshape(E, slots, toks)
    )
    comb = jnp.sum(jnp.where(hit, route_weights[:, :, None], 0.0), axis=1)
    high = lax.reduce_precision(comb, 8, 7)
    comb2 = jnp.concatenate([high, comb - high], axis=0).astype(jnp.bfloat16)
    rows = toks * heads
    bf, f32 = jnp.bfloat16, jnp.float32
    vm = pl.BlockSpec(memory_space=pltpu.VMEM)
    hbm = pl.BlockSpec(memory_space=pl.ANY)
    dma = pltpu.SemaphoreType.DMA
    attended, mixed = pl.pallas_call(
        functools.partial(layer_kernel, E),
        out_shape=(
            jax.ShapeDtypeStruct((rows, LAT), bf),
            jax.ShapeDtypeStruct((toks, D), bf),
        ),
        in_specs=[hbm, vm, vm, vm, vm, hbm, hbm, hbm],
        out_specs=(vm, vm),
        scratch_shapes=[
            pltpu.VMEM((rows, qw), bf),
            pltpu.VMEM((D, ff), bf),
            pltpu.VMEM((D, ff), bf),
            pltpu.VMEM((ff, D), bf),
            pltpu.VMEM((n_ctx, slots, D), bf),
            pltpu.VMEM((E, slots, D), bf),
            pltpu.VMEM((n_ctx, slots, D), bf),
            pltpu.VMEM((2 * E, slots, D), bf),
            pltpu.VMEM((E, slots, D), bf),
            pltpu.VMEM((E, slots, D), bf),
            pltpu.VMEM((n_ctx, toks, qw), bf),
            pltpu.VMEM((rows, LAT), f32),
            pltpu.VMEM((rows, 1), f32),
            pltpu.VMEM((rows, 1), f32),
            dma((4,)),
        ]
        + [dma((E,))] * 8
        + [dma((2 * E,))] * 6
        + [dma((E,))] * 4,
        compiler_params=pltpu.CompilerParams(
            collective_id=0, has_side_effects=True, vmem_limit_bytes=60 * 1024 * 1024
        ),
    )(
        queries.reshape(rows, qw), latent_keys, hidden, sel, comb2,
        w_gate[0], w_up[0], w_down[0],
    )
    return (attended.reshape(toks, heads, LAT), mixed)


def solution(mesh):
    in_specs = (
        P(("group", "ctx"), None, None),
        P(("group", "ctx"), None),
        P(("group", "ctx"), None),
        P(("group", "ctx"), None),
        P(("group", "ctx"), None),
        P("ctx", None, None),
        P("ctx", None, None),
        P("ctx", None, None),
    )
    out_specs = (P(("group", "ctx"), None, None), P(("group", "ctx"), None))
    return jax.shard_map(
        per_device, mesh=mesh, in_specs=in_specs, out_specs=out_specs, check_vma=False
    )
```

```python
import functools
import math

import jax
import jax.numpy as jnp
from jax import lax
from jax.experimental import pallas as pl
from jax.experimental.pallas import tpu as pltpu
from jax.sharding import PartitionSpec as P

LAT = 256
ROPE = 64
NOPE_DIM = 128
SPLIT = 4
TOPK = 2
ROWS = 512


PARTS = 2
AHEAD = 1


def layer_kernel(
    experts, slots, q_hbm, keys_ref, hid_ref, routes_ref, routes_t_ref, weights_ref,
    wg_hbm, wu_hbm, wd_hbm,
    att_ref, mix_ref,
    q_v, wg, wu, wd, recv, own, part, cbuf, xbuf, ret, kbuf, acc, m_ref, l_ref,
    local_sem, sz, rz, sx, rx, srx, rrx, srz, rrz, sc, rc, src_, rrc,
    skz, rkz, skx, rkx, skc, rkc,
):
    E = experts
    toks = keys_ref.shape[0]
    D = hid_ref.shape[1]
    dh = D // PARTS
    row_total = q_v.shape[0]
    heads = row_total // toks
    me = lax.axis_index("ctx")
    e = me // SPLIT
    s = me % SPLIT
    p = s // 2
    c = s % 2
    s_x = (1 - p) * 2 + c
    dev_x = e * SPLIT + s_x
    dev_c = e * SPLIT + p * 2 + (1 - c)

    def remote(src, dst, ssem, rsem, dev):
        return pltpu.make_async_remote_copy(
            src_ref=src, dst_ref=dst, send_sem=ssem, recv_sem=rsem,
            device_id={"ctx": dev}, device_id_type=pl.DeviceIdType.MESH,
        )

    barrier = pltpu.get_barrier_semaphore()

    def greet(k, _):
        pl.semaphore_signal(
            barrier, inc=1, device_id={"ctx": (e + k) % E * SPLIT + s},
            device_id_type=pl.DeviceIdType.MESH,
        )
        return 0

    lax.fori_loop(1, E, greet, 0)
    for dev in (dev_x, dev_c):
        pl.semaphore_signal(
            barrier, inc=1, device_id={"ctx": dev}, device_id_type=pl.DeviceIdType.MESH
        )
    loads = [
        pltpu.make_async_copy(q_hbm, q_v, local_sem.at[0]),
        pltpu.make_async_copy(wg_hbm, wg, local_sem.at[1]),
        pltpu.make_async_copy(wu_hbm, wu, local_sem.at[2]),
        pltpu.make_async_copy(wd_hbm, wd, local_sem.at[3]),
    ]
    for load in loads:
        load.start()
    kbuf[me] = keys_ref[...]

    older = lax.broadcasted_iota(jnp.int32, (toks, toks), 1)
    newer = lax.broadcasted_iota(jnp.int32, (toks, toks), 0)
    slot_col, slot_row = [], []
    for k in range(TOPK):
        col_id, row_id = routes_ref[:, k : k + 1], routes_t_ref[k : k + 1, :]
        col_rank = jnp.zeros((toks, 1), jnp.int32)
        row_rank = jnp.zeros((1, toks), jnp.int32)
        for j in range(TOPK):
            before = (routes_t_ref[j : j + 1, :] == col_id) & (
                older * TOPK + j < newer * TOPK + k
            )
            col_rank += jnp.sum(before.astype(jnp.int32), axis=1, keepdims=True)
            before = (routes_ref[:, j : j + 1] == row_id) & (
                newer * TOPK + j < older * TOPK + k
            )
            row_rank += jnp.sum(before.astype(jnp.int32), axis=0, keepdims=True)
        slot_col.append(col_id * slots + col_rank)
        slot_row.append(row_id * slots + row_rank)

    def select(t):
        place = t * slots + lax.broadcasted_iota(jnp.int32, (slots, toks), 0)
        hit = jnp.where(place == slot_row[0], 1.0, 0.0)
        for k in range(1, TOPK):
            hit += jnp.where(place == slot_row[k], 1.0, 0.0)
        return hit.astype(jnp.bfloat16)

    pl.semaphore_wait(barrier, E + 1)

    def copy_z(t, i_src, h):
        return remote(
            own.at[h, t], recv.at[h, me], sz.at[h, t], rz.at[h, i_src], t * SPLIT + s
        )

    def copy_kz(t, i_src):
        return remote(kbuf.at[me], kbuf.at[me], skz.at[t], rkz.at[i_src], t * SPLIT + s)

    def copy_x(g, h):
        b = g * SPLIT + s
        return remote(recv.at[h, b], recv.at[h, b], sx.at[h, g], rx.at[h, g], dev_x)

    def copy_kx(g):
        b = g * SPLIT + s
        return remote(kbuf.at[b], kbuf.at[b], skx.at[g], rkx.at[g], dev_x)

    def copy_c(g, far, h):
        b = g * SPLIT + (s_x if far else s)
        return remote(
            recv.at[h, b], recv.at[h, b], sc.at[h, 2 * g + far], rc.at[h, 2 * g + far], dev_c
        )

    def copy_kc(g, far):
        b = g * SPLIT + (s_x if far else s)
        return remote(kbuf.at[b], kbuf.at[b], skc.at[2 * g + far], rkc.at[2 * g + far], dev_c)

    def copy_rc(g, q, h):
        return remote(
            part.at[h, g * SPLIT + 2 * q + (1 - c)], cbuf.at[h, 2 * g + q],
            src_.at[h, 2 * g + q], rrc.at[h, 2 * g + q], dev_c,
        )

    def copy_rx(g, h):
        return remote(
            part.at[h, g * SPLIT + s_x], xbuf.at[h, g], srx.at[h, g], rrx.at[h, g], dev_x
        )

    def copy_rz(g, i_src, h):
        return remote(
            part.at[h, g * SPLIT + s], ret.at[h, e], srz.at[h, g], rrz.at[h, i_src],
            g * SPLIT + s,
        )

    def send_keys(k, _):
        copy_kz((e + k) % E, e).start()
        return 0

    lax.fori_loop(1, E, send_keys, 0)
    copy_kx(e).start()
    copy_kc(e, 0).start()

    def dispatch(k):
        t = (e + k) % E
        mine = select(t)
        for h in range(PARTS):
            own[h, t] = jnp.dot(
                mine, hid_ref[:, h * dh : (h + 1) * dh], preferred_element_type=jnp.float32
            ).astype(jnp.bfloat16)
            copy_z(t, e, h).start()

    @pl.when(E > 1)
    def _():
        dispatch(1)

    mine = select(e)
    for h in range(PARTS):
        recv[h, me] = jnp.dot(
            mine, hid_ref[:, h * dh : (h + 1) * dh], preferred_element_type=jnp.float32
        ).astype(jnp.bfloat16)
        copy_x(e, h).start()
        copy_c(e, 0, h).start()

    def early(k, _):
        dispatch(k)
        return 0

    lax.fori_loop(2, min(E, 1 + AHEAD), early, 0)

    def source(k):
        return (e + E - k) % E

    def relay_near(k):
        g = source(k)
        for h in range(PARTS):
            copy_z(g, g, h).wait_recv()
            copy_x(g, h).start()
            copy_c(g, 0, h).start()

        @pl.when(k + AHEAD < E)
        def _():
            dispatch(k + AHEAD)

    def relay_far(k):
        g = source(k)
        for h in range(PARTS):
            copy_x(g, h).wait_recv()
            copy_c(g, 1, h).start()

    def compute(k):
        g = source(k)

        @pl.when(k == 0)
        def _():
            for load in loads[1:]:
                load.wait()

        gate = jnp.zeros((SPLIT * slots, wg.shape[1]), jnp.float32)
        upper = gate
        for h in range(PARTS):
            copy_c(g, 0, h).wait_recv()
            copy_c(g, 1, h).wait_recv()
            rows = recv[h, pl.ds(g * SPLIT, SPLIT)].reshape(SPLIT * slots, dh)
            cut = slice(h * dh, (h + 1) * dh)
            gate += jnp.dot(rows, wg[cut, :], preferred_element_type=jnp.float32)
            upper += jnp.dot(rows, wu[cut, :], preferred_element_type=jnp.float32)
        units = (gate / (1.0 + jnp.exp(-gate)) * upper).astype(jnp.bfloat16)
        width = dh // 2
        for h in range(PARTS):
            for start in range(0, dh, width):
                piece = jnp.dot(
                    units, wd[:, h * dh + start : h * dh + start + width],
                    preferred_element_type=jnp.float32,
                )
                part[h, pl.ds(g * SPLIT, SPLIT), :, start : start + width] = piece.astype(
                    jnp.bfloat16
                ).reshape(SPLIT, slots, width)
            copy_rc(g, 1 - p, h).start()
            copy_rc(g, p, h).start()

    factor = math.log2(math.e) / math.sqrt(NOPE_DIM + ROPE)

    def attend(k):
        g = source(k)
        copy_kc(g, 0).wait_recv()
        copy_kc(g, 1).wait_recv()

        def scores_of(r):
            keys = kbuf[pl.ds(g * SPLIT, SPLIT)].reshape(SPLIT * toks, LAT + ROPE)
            sc_ = lax.dot_general(
                q_v[pl.ds(r, ROWS)], keys, (((1,), (1,)), ((), ())),
                preferred_element_type=jnp.float32,
            )
            return sc_, keys[:, :LAT]

        @pl.when(k == 0)
        def _():
            loads[0].wait()

            def chunk(i, _):
                r = pl.multiple_of(i * ROWS, ROWS)
                sc_, vals = scores_of(r)
                tok = s * toks + (r + lax.broadcasted_iota(jnp.int32, sc_.shape, 0)) // heads
                col = lax.broadcasted_iota(jnp.int32, sc_.shape, 1)
                sc_ = jnp.where(col <= tok, sc_, -jnp.inf)
                m = jnp.max(sc_, axis=1, keepdims=True)
                ex = jnp.exp2((sc_ - m) * factor)
                m_ref[pl.ds(r, ROWS)] = m
                l_ref[pl.ds(r, ROWS)] = jnp.sum(ex, axis=1, keepdims=True)
                acc[pl.ds(r, ROWS)] = jnp.dot(
                    ex.astype(jnp.bfloat16), vals, preferred_element_type=jnp.float32
                )
                return 0

            lax.fori_loop(0, row_total // ROWS, chunk, 0)

        @pl.when(k > 0)
        def _():
            def chunk(i, _):
                r = pl.multiple_of(i * ROWS, ROWS)
                sc_, vals = scores_of(r)
                old = m_ref[pl.ds(r, ROWS)]
                m = jnp.maximum(old, jnp.max(sc_, axis=1, keepdims=True))
                ex = jnp.exp2((sc_ - m) * factor)
                fade = jnp.exp2((old - m) * factor)
                m_ref[pl.ds(r, ROWS)] = m
                l_ref[pl.ds(r, ROWS)] = l_ref[pl.ds(r, ROWS)] * fade + jnp.sum(
                    ex, axis=1, keepdims=True
                )
                acc[pl.ds(r, ROWS)] = acc[pl.ds(r, ROWS)] * fade + jnp.dot(
                    ex.astype(jnp.bfloat16), vals, preferred_element_type=jnp.float32
                )
                return 0

            lax.fori_loop(0, row_total // ROWS, chunk, 0)

    def sum_cores(k):
        g = source(k)
        b = g * SPLIT + s_x
        for h in range(PARTS):
            copy_rc(g, 1 - p, h).wait_recv()
            part[h, b] = (
                part[h, b].astype(jnp.float32)
                + cbuf[h, 2 * g + (1 - p)].astype(jnp.float32)
            ).astype(jnp.bfloat16)
            copy_rx(g, h).start()

    def sum_chips(k):
        g = source(k)
        b = g * SPLIT + s
        for h in range(PARTS):
            copy_rc(g, p, h).wait_recv()
            copy_rx(g, h).wait_recv()
            total = (
                part[h, b].astype(jnp.float32)
                + cbuf[h, 2 * g + p].astype(jnp.float32)
                + xbuf[h, g].astype(jnp.float32)
            ).astype(jnp.bfloat16)

            @pl.when(k == 0)
            def _():
                ret[h, e] = total

            @pl.when(k > 0)
            def _():
                part[h, b] = total
                copy_rz(g, e, h).start()

    def relay_keys(k, _):
        g = source(k)

        @pl.when(k > 0)
        def _():
            copy_kz(g, g).wait_recv()
            copy_kx(g).start()
            copy_kc(g, 0).start()

        copy_kx(g).wait_recv()
        copy_kc(g, 1).start()
        return 0

    lax.fori_loop(0, E, relay_keys, 0)
    relay_far(0)
    attend(0)
    compute(0)

    def step(k, _):
        relay_near(k)
        sum_cores(k - 1)

        @pl.when(k <= e)
        def _():
            attend(k)

        relay_far(k)
        sum_chips(k - 1)
        compute(k)
        return 0

    lax.fori_loop(1, E, step, 0)
    sum_cores(E - 1)
    sum_chips(E - 1)

    def finish(i, _):
        r = pl.multiple_of(i * ROWS, ROWS)
        att_ref[pl.ds(r, ROWS)] = (acc[pl.ds(r, ROWS)] / l_ref[pl.ds(r, ROWS)]).astype(
            jnp.bfloat16
        )
        return 0

    lax.fori_loop(0, row_total // ROWS, finish, 0)

    def unread(k, _):
        g = source(k)
        copy_kc(g, 0).wait_recv()
        copy_kc(g, 1).wait_recv()
        return 0

    lax.fori_loop(e + 1, E, unread, 0)

    def sent(g, _):
        @pl.when(g != e)
        def _():
            copy_kz(g, e).wait_send()
            for h in range(PARTS):
                copy_z(g, e, h).wait_send()

        copy_kx(g).wait_send()
        for far in range(2):
            copy_kc(g, far).wait_send()
        for h in range(PARTS):
            copy_x(g, h).wait_send()
            copy_rx(g, h).wait_send()
            for far in range(2):
                copy_c(g, far, h).wait_send()
                copy_rc(g, far, h).wait_send()
        return 0

    lax.fori_loop(0, E, sent, 0)

    place = lax.broadcasted_iota(jnp.int32, (toks, E * slots), 1)
    comb = jnp.where(place == slot_col[0], weights_ref[:, 0:1], 0.0)
    for k in range(1, TOPK):
        comb += jnp.where(place == slot_col[k], weights_ref[:, k : k + 1], 0.0)
    high = comb.astype(jnp.bfloat16)
    low = (comb - high.astype(jnp.float32)).astype(jnp.bfloat16)
    both = jnp.concatenate([high, low], axis=0)
    for h in range(PARTS):

        def arrive(k, _):
            g = source(k)
            copy_rz(g, g, h).wait_recv()
            return 0

        lax.fori_loop(1, E, arrive, 0)
        out = jnp.dot(
            both, ret[h].reshape(E * slots, dh), preferred_element_type=jnp.float32
        )
        mix_ref[:, h * dh : (h + 1) * dh] = (out[:toks] + out[toks:]).astype(jnp.bfloat16)

    def returned(g, _):
        @pl.when(g != e)
        def _():
            for h in range(PARTS):
                copy_rz(g, e, h).wait_send()

        return 0

    lax.fori_loop(0, E, returned, 0)


def per_device(queries, latent_keys, hidden, routes, route_weights, w_gate, w_up, w_down):
    toks, heads, qw = queries.shape
    D = hidden.shape[1]
    ff = w_gate.shape[2]
    n_ctx = lax.axis_size("ctx")
    E = n_ctx // SPLIT
    most = toks * TOPK * 5 // (4 * E)
    slots = -(-most // 8) * 8
    rows = toks * heads
    dh = D // PARTS
    bf, f32 = jnp.bfloat16, jnp.float32
    vm = pl.BlockSpec(memory_space=pltpu.VMEM)
    hbm = pl.BlockSpec(memory_space=pl.ANY)
    dma = pltpu.SemaphoreType.DMA
    attended, mixed = pl.pallas_call(
        functools.partial(layer_kernel, E, slots),
        out_shape=(
            jax.ShapeDtypeStruct((rows, LAT), bf),
            jax.ShapeDtypeStruct((toks, D), bf),
        ),
        in_specs=[hbm, vm, vm, vm, vm, vm, hbm, hbm, hbm],
        out_specs=(vm, vm),
        scratch_shapes=[
            pltpu.VMEM((rows, qw), bf),
            pltpu.VMEM((D, ff), bf),
            pltpu.VMEM((D, ff), bf),
            pltpu.VMEM((ff, D), bf),
            pltpu.VMEM((PARTS, n_ctx, slots, dh), bf),
            pltpu.VMEM((PARTS, E, slots, dh), bf),
            pltpu.VMEM((PARTS, n_ctx, slots, dh), bf),
            pltpu.VMEM((PARTS, 2 * E, slots, dh), bf),
            pltpu.VMEM((PARTS, E, slots, dh), bf),
            pltpu.VMEM((PARTS, E, slots, dh), bf),
            pltpu.VMEM((n_ctx, toks, qw), bf),
            pltpu.VMEM((rows, LAT), f32),
            pltpu.VMEM((rows, 1), f32),
            pltpu.VMEM((rows, 1), f32),
            dma((4,)),
        ]
        + [dma((PARTS, E))] * 8
        + [dma((PARTS, 2 * E))] * 4
        + [dma((E,))] * 4
        + [dma((2 * E,))] * 2,
        compiler_params=pltpu.CompilerParams(
            collective_id=0, has_side_effects=True, vmem_limit_bytes=60 * 1024 * 1024
        ),
    )(
        queries.reshape(rows, qw), latent_keys, hidden, routes, routes.T, route_weights,
        w_gate[0], w_up[0], w_down[0],
    )
    return (attended.reshape(toks, heads, LAT), mixed)


def solution(mesh):
    in_specs = (
        P(("group", "ctx"), None, None),
        P(("group", "ctx"), None),
        P(("group", "ctx"), None),
        P(("group", "ctx"), None),
        P(("group", "ctx"), None),
        P("ctx", None, None),
        P("ctx", None, None),
        P("ctx", None, None),
    )
    out_specs = (P(("group", "ctx"), None, None), P(("group", "ctx"), None))
    return jax.shard_map(
        per_device, mesh=mesh, in_specs=in_specs, out_specs=out_specs, check_vma=False
    )
```

```python
import functools
import math

import jax
import jax.numpy as jnp
from jax import lax
from jax.experimental import pallas as pl
from jax.experimental.pallas import tpu as pltpu
from jax.sharding import PartitionSpec as P

LAT = 256
ROPE = 64
NOPE_DIM = 128
SPLIT = 4
TOPK = 2
ROWS = 512


PARTS = 2
AHEAD = 1


def layer_kernel(
    experts, slots, q_hbm, keys_ref, hid_ref, routes_ref, routes_t_ref, weights_ref,
    wg_hbm, wu_hbm, wd_hbm,
    att_ref, mix_ref,
    q_v, wg, wu, wd, recv, own, part, cbuf, xbuf, ret, kbuf, acc, m_ref, l_ref,
    local_sem, sz, rz, sx, rx, srx, rrx, srz, rrz, sc, rc, src_, rrc,
    skz, rkz, skx, rkx, skc, rkc,
):
    E = experts
    toks = keys_ref.shape[0]
    D = hid_ref.shape[1]
    dh = D // PARTS
    row_total = q_v.shape[0]
    heads = row_total // toks
    me = lax.axis_index("ctx")
    e = me // SPLIT
    s = me % SPLIT
    p = s // 2
    c = s % 2
    s_x = (1 - p) * 2 + c
    dev_x = e * SPLIT + s_x
    dev_c = e * SPLIT + p * 2 + (1 - c)

    def remote(src, dst, ssem, rsem, dev):
        return pltpu.make_async_remote_copy(
            src_ref=src, dst_ref=dst, send_sem=ssem, recv_sem=rsem,
            device_id={"ctx": dev}, device_id_type=pl.DeviceIdType.MESH,
        )

    barrier = pltpu.get_barrier_semaphore()

    def greet(k, _):
        pl.semaphore_signal(
            barrier, inc=1, device_id={"ctx": (e + k) % E * SPLIT + s},
            device_id_type=pl.DeviceIdType.MESH,
        )
        return 0

    lax.fori_loop(1, E, greet, 0)
    for dev in (dev_x, dev_c):
        pl.semaphore_signal(
            barrier, inc=1, device_id={"ctx": dev}, device_id_type=pl.DeviceIdType.MESH
        )
    loads = [
        pltpu.make_async_copy(q_hbm, q_v, local_sem.at[0]),
        pltpu.make_async_copy(wg_hbm, wg, local_sem.at[1]),
        pltpu.make_async_copy(wu_hbm, wu, local_sem.at[2]),
        pltpu.make_async_copy(wd_hbm, wd, local_sem.at[3]),
    ]
    for load in loads:
        load.start()
    kbuf[me] = keys_ref[...]

    older = lax.broadcasted_iota(jnp.int32, (toks, toks), 1)
    newer = lax.broadcasted_iota(jnp.int32, (toks, toks), 0)
    slot_col, slot_row = [], []
    for k in range(TOPK):
        col_id, row_id = routes_ref[:, k : k + 1], routes_t_ref[k : k + 1, :]
        col_rank = jnp.zeros((toks, 1), jnp.int32)
        row_rank = jnp.zeros((1, toks), jnp.int32)
        for j in range(TOPK):
            before = (routes_t_ref[j : j + 1, :] == col_id) & (
                older * TOPK + j < newer * TOPK + k
            )
            col_rank += jnp.sum(before.astype(jnp.int32), axis=1, keepdims=True)
            before = (routes_ref[:, j : j + 1] == row_id) & (
                newer * TOPK + j < older * TOPK + k
            )
            row_rank += jnp.sum(before.astype(jnp.int32), axis=0, keepdims=True)
        slot_col.append(col_id * slots + col_rank)
        slot_row.append(row_id * slots + row_rank)

    def select(t):
        place = t * slots + lax.broadcasted_iota(jnp.int32, (slots, toks), 0)
        hit = jnp.where(place == slot_row[0], 1.0, 0.0)
        for k in range(1, TOPK):
            hit += jnp.where(place == slot_row[k], 1.0, 0.0)
        return hit.astype(jnp.bfloat16)

    pl.semaphore_wait(barrier, E + 1)

    def copy_z(t, i_src, h):
        return remote(
            own.at[h, t], recv.at[h, me], sz.at[h, t], rz.at[h, i_src], t * SPLIT + s
        )

    def copy_kz(t, i_src):
        return remote(kbuf.at[me], kbuf.at[me], skz.at[t], rkz.at[i_src], t * SPLIT + s)

    def copy_x(g, h):
        b = g * SPLIT + s
        return remote(recv.at[h, b], recv.at[h, b], sx.at[h, g], rx.at[h, g], dev_x)

    def copy_kx(g):
        b = g * SPLIT + s
        return remote(kbuf.at[b], kbuf.at[b], skx.at[g], rkx.at[g], dev_x)

    def copy_c(g, far, h):
        b = g * SPLIT + (s_x if far else s)
        return remote(
            recv.at[h, b], recv.at[h, b], sc.at[h, 2 * g + far], rc.at[h, 2 * g + far], dev_c
        )

    def copy_kc(g, far):
        b = g * SPLIT + (s_x if far else s)
        return remote(kbuf.at[b], kbuf.at[b], skc.at[2 * g + far], rkc.at[2 * g + far], dev_c)

    def copy_rc(g, q, h):
        return remote(
            part.at[h, g * SPLIT + 2 * q + (1 - c)], cbuf.at[h, 2 * g + q],
            src_.at[h, 2 * g + q], rrc.at[h, 2 * g + q], dev_c,
        )

    def copy_rx(g, h):
        return remote(
            part.at[h, g * SPLIT + s_x], xbuf.at[h, g], srx.at[h, g], rrx.at[h, g], dev_x
        )

    def copy_rz(g, i_src, h):
        return remote(
            part.at[h, g * SPLIT + s], ret.at[h, e], srz.at[h, g], rrz.at[h, i_src],
            g * SPLIT + s,
        )

    def send_keys(k, _):
        copy_kz((e + k) % E, e).start()
        return 0

    lax.fori_loop(1, E, send_keys, 0)
    copy_kx(e).start()
    copy_kc(e, 0).start()

    def dispatch(k):
        t = (e + k) % E
        mine = select(t)
        for h in range(PARTS):
            own[h, t] = jnp.dot(
                mine, hid_ref[:, h * dh : (h + 1) * dh], preferred_element_type=jnp.float32
            ).astype(jnp.bfloat16)
            copy_z(t, e, h).start()

    @pl.when(E > 1)
    def _():
        dispatch(1)

    mine = select(e)
    for h in range(PARTS):
        recv[h, me] = jnp.dot(
            mine, hid_ref[:, h * dh : (h + 1) * dh], preferred_element_type=jnp.float32
        ).astype(jnp.bfloat16)
        copy_x(e, h).start()
        copy_c(e, 0, h).start()

    def early(k, _):
        dispatch(k)
        return 0

    lax.fori_loop(2, min(E, 1 + AHEAD), early, 0)

    def source(k):
        return (e + E - k) % E

    def relay_near(k):
        g = source(k)
        for h in range(PARTS):
            copy_z(g, g, h).wait_recv()
            copy_x(g, h).start()
            copy_c(g, 0, h).start()

        @pl.when(k + AHEAD < E)
        def _():
            dispatch(k + AHEAD)

    def relay_far(k):
        g = source(k)
        for h in range(PARTS):
            copy_x(g, h).wait_recv()
            copy_c(g, 1, h).start()

    def compute(k):
        g = source(k)

        @pl.when(k == 0)
        def _():
            for load in loads[1:]:
                load.wait()

        gate = jnp.zeros((SPLIT * slots, wg.shape[1]), jnp.float32)
        upper = gate
        for h in range(PARTS):
            copy_c(g, 0, h).wait_recv()
            copy_c(g, 1, h).wait_recv()
            rows = recv[h, pl.ds(g * SPLIT, SPLIT)].reshape(SPLIT * slots, dh)
            cut = slice(h * dh, (h + 1) * dh)
            gate += jnp.dot(rows, wg[cut, :], preferred_element_type=jnp.float32)
            upper += jnp.dot(rows, wu[cut, :], preferred_element_type=jnp.float32)
        units = (gate / (1.0 + jnp.exp(-gate)) * upper).astype(jnp.bfloat16)
        width = dh // 2
        for h in range(PARTS):
            for start in range(0, dh, width):
                piece = jnp.dot(
                    units, wd[:, h * dh + start : h * dh + start + width],
                    preferred_element_type=jnp.float32,
                )
                part[h, pl.ds(g * SPLIT, SPLIT), :, start : start + width] = piece.astype(
                    jnp.bfloat16
                ).reshape(SPLIT, slots, width)
            copy_rc(g, 1 - p, h).start()
            copy_rc(g, p, h).start()

    factor = math.log2(math.e) / math.sqrt(NOPE_DIM + ROPE)

    def attend(k):
        g = source(k)
        copy_kc(g, 0).wait_recv()
        copy_kc(g, 1).wait_recv()

        def scores_of(r):
            keys = kbuf[pl.ds(g * SPLIT, SPLIT)].reshape(SPLIT * toks, LAT + ROPE)
            sc_ = lax.dot_general(
                q_v[pl.ds(r, ROWS)], keys, (((1,), (1,)), ((), ())),
                preferred_element_type=jnp.float32,
            )
            return sc_, keys[:, :LAT]

        @pl.when(k == 0)
        def _():
            loads[0].wait()

            def chunk(i, _):
                r = pl.multiple_of(i * ROWS, ROWS)
                sc_, vals = scores_of(r)
                tok = s * toks + (r + lax.broadcasted_iota(jnp.int32, sc_.shape, 0)) // heads
                col = lax.broadcasted_iota(jnp.int32, sc_.shape, 1)
                sc_ = jnp.where(col <= tok, sc_, -jnp.inf)
                m = jnp.max(sc_, axis=1, keepdims=True)
                ex = jnp.exp2((sc_ - m) * factor)
                m_ref[pl.ds(r, ROWS)] = m
                l_ref[pl.ds(r, ROWS)] = jnp.sum(ex, axis=1, keepdims=True)
                acc[pl.ds(r, ROWS)] = jnp.dot(
                    ex.astype(jnp.bfloat16), vals, preferred_element_type=jnp.float32
                )
                return 0

            lax.fori_loop(0, row_total // ROWS, chunk, 0)

        @pl.when(k > 0)
        def _():
            def chunk(i, _):
                r = pl.multiple_of(i * ROWS, ROWS)
                sc_, vals = scores_of(r)
                old = m_ref[pl.ds(r, ROWS)]
                m = jnp.maximum(old, jnp.max(sc_, axis=1, keepdims=True))
                ex = jnp.exp2((sc_ - m) * factor)
                fade = jnp.exp2((old - m) * factor)
                m_ref[pl.ds(r, ROWS)] = m
                l_ref[pl.ds(r, ROWS)] = l_ref[pl.ds(r, ROWS)] * fade + jnp.sum(
                    ex, axis=1, keepdims=True
                )
                acc[pl.ds(r, ROWS)] = acc[pl.ds(r, ROWS)] * fade + jnp.dot(
                    ex.astype(jnp.bfloat16), vals, preferred_element_type=jnp.float32
                )
                return 0

            lax.fori_loop(0, row_total // ROWS, chunk, 0)

    def sum_cores(k):
        g = source(k)
        b = g * SPLIT + s_x
        for h in range(PARTS):
            copy_rc(g, 1 - p, h).wait_recv()
            part[h, b] = (
                part[h, b].astype(jnp.float32)
                + cbuf[h, 2 * g + (1 - p)].astype(jnp.float32)
            ).astype(jnp.bfloat16)
            copy_rx(g, h).start()

    def sum_chips(k):
        g = source(k)
        b = g * SPLIT + s
        for h in range(PARTS):
            copy_rc(g, p, h).wait_recv()
            copy_rx(g, h).wait_recv()
            total = (
                part[h, b].astype(jnp.float32)
                + cbuf[h, 2 * g + p].astype(jnp.float32)
                + xbuf[h, g].astype(jnp.float32)
            ).astype(jnp.bfloat16)

            @pl.when(k == 0)
            def _():
                ret[h, e] = total

            @pl.when(k > 0)
            def _():
                part[h, b] = total
                copy_rz(g, e, h).start()

    def relay_keys(k, _):
        g = source(k)

        @pl.when(k > 0)
        def _():
            copy_kz(g, g).wait_recv()
            copy_kx(g).start()
            copy_kc(g, 0).start()

        copy_kx(g).wait_recv()
        copy_kc(g, 1).start()
        return 0

    lax.fori_loop(0, E, relay_keys, 0)
    relay_far(0)
    attend(0)
    compute(0)

    def step(k, _):
        relay_near(k)

        @pl.when(k <= e)
        def _():
            attend(k)

        relay_far(k)
        sum_cores(k - 1)
        compute(k)
        sum_chips(k - 1)
        return 0

    lax.fori_loop(1, E, step, 0)
    sum_cores(E - 1)
    sum_chips(E - 1)

    def finish(i, _):
        r = pl.multiple_of(i * ROWS, ROWS)
        att_ref[pl.ds(r, ROWS)] = (acc[pl.ds(r, ROWS)] / l_ref[pl.ds(r, ROWS)]).astype(
            jnp.bfloat16
        )
        return 0

    lax.fori_loop(0, row_total // ROWS, finish, 0)

    def unread(k, _):
        g = source(k)
        copy_kc(g, 0).wait_recv()
        copy_kc(g, 1).wait_recv()
        return 0

    lax.fori_loop(e + 1, E, unread, 0)

    def sent(g, _):
        @pl.when(g != e)
        def _():
            copy_kz(g, e).wait_send()
            for h in range(PARTS):
                copy_z(g, e, h).wait_send()

        copy_kx(g).wait_send()
        for far in range(2):
            copy_kc(g, far).wait_send()
        for h in range(PARTS):
            copy_x(g, h).wait_send()
            copy_rx(g, h).wait_send()
            for far in range(2):
                copy_c(g, far, h).wait_send()
                copy_rc(g, far, h).wait_send()
        return 0

    lax.fori_loop(0, E, sent, 0)

    place = lax.broadcasted_iota(jnp.int32, (toks, E * slots), 1)
    comb = jnp.where(place == slot_col[0], weights_ref[:, 0:1], 0.0)
    for k in range(1, TOPK):
        comb += jnp.where(place == slot_col[k], weights_ref[:, k : k + 1], 0.0)
    high = comb.astype(jnp.bfloat16)
    low = (comb - high.astype(jnp.float32)).astype(jnp.bfloat16)
    both = jnp.concatenate([high, low], axis=0)
    for h in range(PARTS):

        def arrive(k, _):
            g = source(k)
            copy_rz(g, g, h).wait_recv()
            return 0

        lax.fori_loop(1, E, arrive, 0)
        out = jnp.dot(
            both, ret[h].reshape(E * slots, dh), preferred_element_type=jnp.float32
        )
        mix_ref[:, h * dh : (h + 1) * dh] = (out[:toks] + out[toks:]).astype(jnp.bfloat16)

    def returned(g, _):
        @pl.when(g != e)
        def _():
            for h in range(PARTS):
                copy_rz(g, e, h).wait_send()

        return 0

    lax.fori_loop(0, E, returned, 0)


def per_device(queries, latent_keys, hidden, routes, route_weights, w_gate, w_up, w_down):
    toks, heads, qw = queries.shape
    D = hidden.shape[1]
    ff = w_gate.shape[2]
    n_ctx = lax.axis_size("ctx")
    E = n_ctx // SPLIT
    most = toks * TOPK * 5 // (4 * E)
    slots = -(-most // 8) * 8
    rows = toks * heads
    dh = D // PARTS
    bf, f32 = jnp.bfloat16, jnp.float32
    vm = pl.BlockSpec(memory_space=pltpu.VMEM)
    hbm = pl.BlockSpec(memory_space=pl.ANY)
    dma = pltpu.SemaphoreType.DMA
    attended, mixed = pl.pallas_call(
        functools.partial(layer_kernel, E, slots),
        out_shape=(
            jax.ShapeDtypeStruct((rows, LAT), bf),
            jax.ShapeDtypeStruct((toks, D), bf),
        ),
        in_specs=[hbm, vm, vm, vm, vm, vm, hbm, hbm, hbm],
        out_specs=(vm, vm),
        scratch_shapes=[
            pltpu.VMEM((rows, qw), bf),
            pltpu.VMEM((D, ff), bf),
            pltpu.VMEM((D, ff), bf),
            pltpu.VMEM((ff, D), bf),
            pltpu.VMEM((PARTS, n_ctx, slots, dh), bf),
            pltpu.VMEM((PARTS, E, slots, dh), bf),
            pltpu.VMEM((PARTS, n_ctx, slots, dh), bf),
            pltpu.VMEM((PARTS, 2 * E, slots, dh), bf),
            pltpu.VMEM((PARTS, E, slots, dh), bf),
            pltpu.VMEM((PARTS, E, slots, dh), bf),
            pltpu.VMEM((n_ctx, toks, qw), bf),
            pltpu.VMEM((rows, LAT), f32),
            pltpu.VMEM((rows, 1), f32),
            pltpu.VMEM((rows, 1), f32),
            dma((4,)),
        ]
        + [dma((PARTS, E))] * 8
        + [dma((PARTS, 2 * E))] * 4
        + [dma((E,))] * 4
        + [dma((2 * E,))] * 2,
        compiler_params=pltpu.CompilerParams(
            collective_id=0, has_side_effects=True, vmem_limit_bytes=60 * 1024 * 1024
        ),
    )(
        queries.reshape(rows, qw), latent_keys, hidden, routes, routes.T, route_weights,
        w_gate[0], w_up[0], w_down[0],
    )
    return (attended.reshape(toks, heads, LAT), mixed)


def solution(mesh):
    in_specs = (
        P(("group", "ctx"), None, None),
        P(("group", "ctx"), None),
        P(("group", "ctx"), None),
        P(("group", "ctx"), None),
        P(("group", "ctx"), None),
        P("ctx", None, None),
        P("ctx", None, None),
        P("ctx", None, None),
    )
    out_specs = (P(("group", "ctx"), None, None), P(("group", "ctx"), None))
    return jax.shard_map(
        per_device, mesh=mesh, in_specs=in_specs, out_specs=out_specs, check_vma=False
    )
```
